256 devices in a mesh: grp: 16 (over x, z_hi), rep: 16 (over y, z_lo, core).
Axes of the slice: x: 4, y: 4, z: 8 (z_hi: 4, z_lo: 2; z = z_hi * 2 + z_lo), core: 2. Of those that a mesh axis runs over, the one named last changes fastest.
Arguments:
- trainer_gate: bfloat16 [6, 7168, 2048], P(None, ('rep', 'grp')), may hold values from -1 to 1
- expert_of_slot: int32 [6], replicated, may hold values from 0 to 5, each once
Outputs:
- rollout_gate: bfloat16 [6, 7168, 2048], P(None, None, 'grp')
- block_scales: bfloat16 [6, 56, 16], P(None, None, 'grp')
The draws below stay inside these ranges and needn't reach their ends.
All inputs are finite; a program needn't handle non-finite values.
Results may differ from the reference program's by a relative error of at most 0.0014.
Values may be sent and summed in bfloat16 or wider, within the bound.
A program may use at most 128 MiB of HBM per device.

```python
import math
import jax
import jax.numpy as jnp

D = 7168
FF = 2048
EXPERTS = 6
QB = 128
QC = 128


def draw_trainer_gate(key, part):
    key = jax.random.fold_in(key, 11)
    first, second, third = jax.random.split(key, 3)
    shape = (EXPERTS, D, FF)
    row_scale = jnp.exp(jax.random.uniform(second, (EXPERTS, D, 1), jnp.float32, 0.0, math.log(10.0)))
    col_scale = jnp.exp(jax.random.uniform(third, (1, 1, FF), jnp.float32, 0.0, math.log(10.0)))
    base = jax.random.truncated_normal(first, -4.0, 4.0, shape, jnp.float32)
    values = base * row_scale * col_scale / (20.0 * math.sqrt(D))
    values = jnp.clip(values, -1.0, 1.0)
    return values.astype(jnp.bfloat16)


def setup_inputs(seed: int = 0) -> dict:
    splits = jax.random.split(jax.random.key(seed), 3)
    return {
        "trainer_gate": draw_trainer_gate(jax.random.fold_in(splits[2], 71), 0),
        "expert_of_slot": jax.random.permutation(splits[1], EXPERTS).astype(jnp.int32),
    }


def reference(trainer_gate, expert_of_slot):
    placed = jnp.take(trainer_gate, expert_of_slot.astype(jnp.int32), axis=0)
    blocks = placed.astype(jnp.float32).reshape(EXPERTS, D // QB, QB, FF // QC, QC)
    largest = jnp.max(jnp.abs(blocks), axis=(2, 4)) + 1e-6
    block_scales = largest.astype(jnp.bfloat16)
    divisor = block_scales.astype(jnp.float32)[:, :, None, :, None]
    rollout_gate = (blocks / divisor).astype(jnp.bfloat16).reshape(EXPERTS, D, FF)
    return rollout_gate, block_scales
```

```python
import functools

import jax
import jax.numpy as jnp
from jax import lax
from jax.experimental import pallas as pl
from jax.experimental.pallas import tpu as pltpu
from jax.sharding import PartitionSpec as P

MESH = pl.DeviceIdType.MESH
EXPERTS, ROWS, FF = 6, 28, 2048
QB = 128
NX, NZ, NY = 4, 4, 4
CHUNKS = 3
SOURCES = 32
SHARE = SOURCES * ROWS
BLOCKS = SHARE // QB
FULL = SHARE + 16
CHIPS = 8

H1 = (0, 448)
H2 = (448, FULL - 448)
A1 = (0, 336)
A2 = (560, FULL - 560)
B = (336, 224)
ALL = (0, FULL)
TAGS = 32


def spread(x_ref, buf, xv, got, rows, load_sem, own_sem, out_sem, in_sem, ssem, rsem):
    g, r = lax.axis_index("grp"), lax.axis_index("rep")
    x, zh = g // NZ, g % NZ
    y, z, c = r // 4, (r // 2) % 2, r % 2

    load = pltpu.make_async_copy(x_ref, xv, load_sem)
    load.start()

    def at(gx, gz, yy, zz, cc):
        return (gx * NZ + gz, (yy * 2 + zz) * 2 + cc)

    up = at(x, zh, (y + 1) % NY, z, c)
    down = at(x, zh, (y + 3) % NY, z, c)
    side = at(x, zh, y, 1 - z, c)
    twin = at(x, zh, y, z, 1 - c)
    exchange = [
        (dx, dz, fc) for dz in (2, 1, 3, 0) for dx in (2, 1, 3, 0) for fc in (0, 1) if (dx, dz, fc) != (0, 0, 0)
    ]

    def peer(dx, dz, fc):
        return (x + dx) % NX, (zh + dz) % NZ, (c + fc) % 2

    barrier = pltpu.get_barrier_semaphore()
    for p in exchange:
        gx, gz, cc = peer(*p)
        pl.semaphore_signal(barrier, inc=1, device_id=at(gx, gz, y, z, cc), device_id_type=MESH)
    for d in (up, down, side):
        pl.semaphore_signal(barrier, inc=1, device_id=d, device_id_type=MESH)
    load.wait()
    mine = c * 16 + g
    for k in range(CHUNKS):
        pltpu.make_async_copy(
            xv.at[c * CHUNKS + k, :, pl.ds(pl.multiple_of(g * QB, QB), QB)], got.at[k, mine], own_sem.at[k]
        ).start()
    pl.semaphore_wait(barrier, len(exchange) + 3)

    for k in range(CHUNKS):
        for p in exchange:
            gx, gz, cc = peer(*p)
            col = pl.multiple_of((gx * NZ + gz) * QB, QB)
            pltpu.make_async_remote_copy(
                src_ref=xv.at[cc * CHUNKS + k, :, pl.ds(col, QB)],
                dst_ref=got.at[k, mine],
                send_sem=out_sem.at[k],
                recv_sem=in_sem.at[k],
                device_id=at(gx, gz, y, z, cc),
                device_id_type=MESH,
            ).start()

    def chip(dy, dz):
        return ((y + dy) % NY) * 2 + (z + dz) % 2

    def copy(k, tag, origin, piece, target, fc=0):
        e = (c + fc) % 2 * CHUNKS + k
        part = buf.at[e, origin, pl.ds(piece[0], piece[1])]
        return pltpu.make_async_remote_copy(
            src_ref=part,
            dst_ref=part,
            send_sem=ssem.at[k, tag],
            recv_sem=rsem.at[k, tag],
            device_id=target,
            device_id_type=MESH,
        )

    plan = {
        0: (chip(0, 0), H1, up),
        1: (chip(0, 0), H2, up),
        2: (chip(0, 0), H2, down),
        3: (chip(0, 0), H1, down),
        4: (chip(0, 0), A1, side),
        5: (chip(0, 0), A2, side),
        6: (chip(0, 0), B, side),
        7: (chip(3, 0), H1, up),
        8: (chip(1, 0), H2, down),
        9: (chip(0, 1), A1, up),
        10: (chip(0, 1), A2, up),
        11: (chip(0, 1), A2, down),
        12: (chip(0, 1), A1, down),
        13: (chip(3, 1), A1, up),
        14: (chip(1, 1), A2, down),
        15: (chip(3, 0), B, side),
        16: (chip(1, 0), B, side),
        17: (chip(2, 0), B, side),
        18: (chip(0, 0), ALL, twin),
        19: (chip(0, 1), ALL, twin),
        20: (chip(3, 0), ALL, twin),
        21: (chip(1, 0), ALL, twin),
        22: (chip(2, 0), ALL, twin),
        23: (chip(3, 1), A1, twin),
        24: (chip(3, 1), A2, twin),
        25: (chip(1, 1), A2, twin),
        26: (chip(1, 1), A1, twin),
        27: (chip(2, 1), A1, twin),
        28: (chip(2, 1), A2, twin),
        29: (chip(3, 1), B, twin),
        30: (chip(1, 1), B, twin),
        31: (chip(2, 1), B, twin),
    }
    came = {
        0: chip(3, 0), 1: chip(3, 0), 2: chip(1, 0), 3: chip(1, 0),
        4: chip(0, 1), 5: chip(0, 1), 6: chip(0, 1),
        7: chip(2, 0), 8: chip(2, 0),
        9: chip(3, 1), 10: chip(3, 1), 11: chip(1, 1), 12: chip(1, 1),
        13: chip(2, 1), 14: chip(2, 1),
        15: chip(3, 1), 16: chip(1, 1), 17: chip(2, 1),
    }

    def send(k, *tags):
        for t in tags:
            copy(k, t, *plan[t]).start()

    def wait(k, *tags):
        for t in tags:
            if t < 18:
                copy(k, t, came[t], plan[t][1], plan[t][2]).wait_recv()
            else:
                copy(k, t, plan[t][0], plan[t][1], plan[t][2], 1).wait_recv()

    def scale(k):
        e, here = c * CHUNKS + k, chip(0, 0)
        pltpu.make_async_copy(got.at[k, 0], got.at[k, 0], own_sem.at[k]).wait()
        pltpu.make_async_copy(got.at[k, pl.ds(0, SOURCES - 1)], got.at[k, pl.ds(0, SOURCES - 1)], in_sem.at[k]).wait()
        for j in range(SOURCES):
            rows[pl.ds(j * ROWS, ROWS), :] = got[k, j].astype(jnp.float32)
        row = lax.broadcasted_iota(jnp.int32, (16, QB), 0)
        scales = jnp.zeros((16, QB), jnp.float32)
        for b in range(BLOCKS):
            v = rows[pl.ds(b * QB, QB), :]
            m = jnp.max(jnp.max(jnp.abs(v), axis=0, keepdims=True), axis=1, keepdims=True) + 1e-06
            s = jnp.broadcast_to(m, (16, QB)).astype(jnp.bfloat16).astype(jnp.float32)
            buf[e, here, pl.ds(b * QB, QB), :] = (v / s[0:1]).astype(jnp.bfloat16)
            scales = jnp.where(row == b, s, scales)
        buf[e, here, pl.ds(SHARE, 16), :] = scales.astype(jnp.bfloat16)
        send(k, 0, 2, 4, 5, 1, 3, 6, 18)

    def early(k):
        wait(k, 0)
        send(k, 7)
        wait(k, 2)
        send(k, 8)
        wait(k, 4)
        send(k, 9, 12)
        wait(k, 5)
        send(k, 11, 10)
        wait(k, 1)
        send(k, 15, 20)
        wait(k, 3)
        send(k, 16, 21)
        wait(k, 6)
        send(k, 19)
        wait(k, 7, 8)
        send(k, 17, 22)

    def late(k):
        wait(k, 9)
        send(k, 13, 23)
        wait(k, 11)
        send(k, 14, 25)
        wait(k, 10)
        send(k, 24)
        wait(k, 12)
        send(k, 26)
        wait(k, 15)
        send(k, 29)
        wait(k, 16)
        send(k, 30)
        wait(k, 13)
        send(k, 27)
        wait(k, 14)
        send(k, 28)
        wait(k, 17)
        send(k, 31)

    scale(0)
    early(0)
    scale(1)
    late(0)
    early(1)
    scale(2)
    late(1)
    early(2)
    late(2)
    for k in range(CHUNKS):
        for t in range(18, TAGS):
            wait(k, t)
        for t in range(TAGS):
            copy(k, t, *plan[t]).wait_send()
        pltpu.make_async_copy(got.at[k, pl.ds(0, SOURCES - 1)], got.at[k, pl.ds(0, SOURCES - 1)], out_sem.at[k]).wait()


def place(slot_ref, buf, out_ref, scale_ref, sem):
    for s in range(EXPERTS):
        e = slot_ref[s]
        for ch in range(CHIPS):
            pltpu.make_async_copy(
                buf.at[e, ch, pl.ds(0, SHARE)], out_ref.at[s, pl.ds(ch * SHARE, SHARE)], sem.at[s, ch]
            ).start()
    for s in range(EXPERTS):
        e = slot_ref[s]
        parts = [buf[e, ch, pl.ds(SHARE, 16), :].astype(jnp.float32)[:BLOCKS] for ch in range(CHIPS)]
        scale_ref[s] = jnp.concatenate(parts, axis=0)[:, 0:1].astype(jnp.bfloat16)
    for s in range(EXPERTS):
        for ch in range(CHIPS):
            pltpu.make_async_copy(
                buf.at[0, ch, pl.ds(0, SHARE)], out_ref.at[s, pl.ds(ch * SHARE, SHARE)], sem.at[s, ch]
            ).wait()


def shards(trainer_gate, expert_of_slot):
    gathered = pl.pallas_call(
        spread,
        out_shape=pltpu.VMEM((EXPERTS, CHIPS, FULL, QB), jnp.bfloat16),
        in_specs=[pl.BlockSpec(memory_space=pl.ANY)],
        out_specs=pl.BlockSpec(memory_space=pltpu.VMEM),
        scratch_shapes=[
            pltpu.VMEM((EXPERTS, ROWS, FF), jnp.bfloat16),
            pltpu.VMEM((CHUNKS, SOURCES, ROWS, QB), jnp.bfloat16),
            pltpu.VMEM((SHARE, QB), jnp.float32),
            pltpu.SemaphoreType.DMA,
            pltpu.SemaphoreType.DMA((CHUNKS,)),
            pltpu.SemaphoreType.DMA((CHUNKS,)),
            pltpu.SemaphoreType.DMA((CHUNKS,)),
            pltpu.SemaphoreType.DMA((CHUNKS, TAGS)),
            pltpu.SemaphoreType.DMA((CHUNKS, TAGS)),
        ],
        compiler_params=pltpu.CompilerParams(collective_id=0, has_side_effects=True, vmem_limit_bytes=20 * 2**20),
        name="spread",
    )(trainer_gate)
    return pl.pallas_call(
        place,
        out_shape=(
            jax.ShapeDtypeStruct((EXPERTS, CHIPS * SHARE, QB), jnp.bfloat16),
            jax.ShapeDtypeStruct((EXPERTS, CHIPS * BLOCKS, 1), jnp.bfloat16),
        ),
        in_specs=[pl.BlockSpec(memory_space=pltpu.SMEM), pl.BlockSpec(memory_space=pltpu.VMEM)],
        out_specs=(pl.BlockSpec(memory_space=pl.ANY), pl.BlockSpec(memory_space=pltpu.VMEM)),
        scratch_shapes=[pltpu.SemaphoreType.DMA((EXPERTS, CHIPS))],
        compiler_params=pltpu.CompilerParams(vmem_limit_bytes=20 * 2**20),
        name="place",
    )(expert_of_slot, gathered)


def solution(mesh):
    return jax.shard_map(
        shards,
        mesh=mesh,
        in_specs=(P(None, ("rep", "grp"), None), P()),
        out_specs=(P(None, None, "grp"), P(None, None, "grp")),
        check_vma=False,
    )
```

```python
import functools

import jax
import jax.numpy as jnp
from jax import lax
from jax.experimental import pallas as pl
from jax.experimental.pallas import tpu as pltpu
from jax.sharding import PartitionSpec as P

MESH = pl.DeviceIdType.MESH
EXPERTS, ROWS, FF = 6, 28, 2048
QB = 128
NX, NZ, NY = 4, 4, 4
CHUNKS = 3
SOURCES = 32
SHARE = SOURCES * ROWS
BLOCKS = SHARE // QB
FULL = SHARE + 16
CHIPS = 8

H1 = (0, 448)
H2 = (448, FULL - 448)
A1 = (0, 288)
A2 = (608, FULL - 608)
B = (288, 320)
ALL = (0, FULL)
TAGS = 32

STEPS = {
    "up 1": ((0,), (7,)),
    "down 2": ((2,), (8,)),
    "up all": ((1,), (15, 20)),
    "down all": ((3,), (16, 21)),
    "side 1": ((4,), (9, 12)),
    "side 2": ((5,), (11, 10)),
    "side all": ((6,), (19,)),
    "far": ((7, 8), (17, 22)),
    "up side 1": ((9,), (13, 23)),
    "down side 2": ((11,), (14, 25)),
    "up side 2": ((10,), (24,)),
    "down side 1": ((12,), (26,)),
    "up between": ((15,), (29,)),
    "down between": ((16,), (30,)),
    "far between": ((17,), (31,)),
    "far side 1": ((13,), (27,)),
    "far side 2": ((14,), (28,)),
}
ORDER = (
    ("scale", 0), ("up 1", 0), ("down 2", 0), ("scale", 1), ("up all", 0), ("down all", 0), ("side 1", 0), ("far", 0),
    ("scale", 2), ("side 2", 0), ("up 1", 1), ("down 2", 1), ("side all", 0), ("side 1", 1), ("up all", 1),
    ("down all", 1), ("side 2", 1), ("up side 1", 0), ("down side 1", 0), ("side all", 1), ("up 1", 2), ("down 2", 2),
    ("up between", 0), ("down between", 0), ("up all", 2), ("down all", 2), ("far between", 0), ("up side 2", 0),
    ("down side 2", 0), ("side 1", 2), ("far", 1), ("side 2", 2), ("up side 1", 1), ("down side 1", 1), ("side all", 2),
    ("up side 2", 1), ("down side 2", 1), ("up between", 1), ("far side 1", 0), ("down between", 1), ("far", 2),
    ("far side 2", 0), ("up between", 2), ("up side 1", 2), ("down side 1", 2), ("down between", 2), ("up side 2", 2),
    ("down side 2", 2), ("far between", 1), ("far side 1", 1), ("far side 2", 1), ("far between", 2),
    ("far side 1", 2), ("far side 2", 2),
)


def spread(x_ref, buf, xv, got, rows, load_sem, own_sem, out_sem, in_sem, ssem, rsem):
    g, r = lax.axis_index("grp"), lax.axis_index("rep")
    x, zh = g // NZ, g % NZ
    y, z, c = r // 4, (r // 2) % 2, r % 2

    load = pltpu.make_async_copy(x_ref, xv, load_sem)
    load.start()

    def at(gx, gz, yy, zz, cc):
        return (gx * NZ + gz, (yy * 2 + zz) * 2 + cc)

    up = at(x, zh, (y + 1) % NY, z, c)
    down = at(x, zh, (y + 3) % NY, z, c)
    side = at(x, zh, y, 1 - z, c)
    twin = at(x, zh, y, z, 1 - c)
    exchange = [
        (dx, dz, fc) for dz in (2, 1, 3, 0) for dx in (2, 1, 3, 0) for fc in (0, 1) if (dx, dz, fc) != (0, 0, 0)
    ]

    def peer(dx, dz, fc):
        return (x + dx) % NX, (zh + dz) % NZ, (c + fc) % 2

    barrier = pltpu.get_barrier_semaphore()
    for p in exchange:
        gx, gz, cc = peer(*p)
        pl.semaphore_signal(barrier, inc=1, device_id=at(gx, gz, y, z, cc), device_id_type=MESH)
    for d in (up, down, side):
        pl.semaphore_signal(barrier, inc=1, device_id=d, device_id_type=MESH)
    load.wait()
    mine = c * 16 + g
    for k in range(CHUNKS):
        pltpu.make_async_copy(
            xv.at[c * CHUNKS + k, :, pl.ds(pl.multiple_of(g * QB, QB), QB)], got.at[k, mine], own_sem.at[k]
        ).start()
    pl.semaphore_wait(barrier, len(exchange) + 3)

    for k in range(CHUNKS):
        for p in exchange:
            gx, gz, cc = peer(*p)
            col = pl.multiple_of((gx * NZ + gz) * QB, QB)
            pltpu.make_async_remote_copy(
                src_ref=xv.at[cc * CHUNKS + k, :, pl.ds(col, QB)],
                dst_ref=got.at[k, mine],
                send_sem=out_sem.at[k],
                recv_sem=in_sem.at[k],
                device_id=at(gx, gz, y, z, cc),
                device_id_type=MESH,
            ).start()

    def chip(dy, dz):
        return ((y + dy) % NY) * 2 + (z + dz) % 2

    def copy(k, tag, origin, piece, target, fc=0):
        e = (c + fc) % 2 * CHUNKS + k
        part = buf.at[e, origin, pl.ds(piece[0], piece[1])]
        return pltpu.make_async_remote_copy(
            src_ref=part,
            dst_ref=part,
            send_sem=ssem.at[k, tag],
            recv_sem=rsem.at[k, tag],
            device_id=target,
            device_id_type=MESH,
        )

    plan = {
        0: (chip(0, 0), H1, up),
        1: (chip(0, 0), H2, up),
        2: (chip(0, 0), H2, down),
        3: (chip(0, 0), H1, down),
        4: (chip(0, 0), A1, side),
        5: (chip(0, 0), A2, side),
        6: (chip(0, 0), B, side),
        7: (chip(3, 0), H1, up),
        8: (chip(1, 0), H2, down),
        9: (chip(0, 1), A1, up),
        10: (chip(0, 1), A2, up),
        11: (chip(0, 1), A2, down),
        12: (chip(0, 1), A1, down),
        13: (chip(3, 1), A1, up),
        14: (chip(1, 1), A2, down),
        15: (chip(3, 0), B, side),
        16: (chip(1, 0), B, side),
        17: (chip(2, 0), B, side),
        18: (chip(0, 0), ALL, twin),
        19: (chip(0, 1), ALL, twin),
        20: (chip(3, 0), ALL, twin),
        21: (chip(1, 0), ALL, twin),
        22: (chip(2, 0), ALL, twin),
        23: (chip(3, 1), A1, twin),
        24: (chip(3, 1), A2, twin),
        25: (chip(1, 1), A2, twin),
        26: (chip(1, 1), A1, twin),
        27: (chip(2, 1), A1, twin),
        28: (chip(2, 1), A2, twin),
        29: (chip(3, 1), B, twin),
        30: (chip(1, 1), B, twin),
        31: (chip(2, 1), B, twin),
    }
    came = {
        0: chip(3, 0), 1: chip(3, 0), 2: chip(1, 0), 3: chip(1, 0),
        4: chip(0, 1), 5: chip(0, 1), 6: chip(0, 1),
        7: chip(2, 0), 8: chip(2, 0),
        9: chip(3, 1), 10: chip(3, 1), 11: chip(1, 1), 12: chip(1, 1),
        13: chip(2, 1), 14: chip(2, 1),
        15: chip(3, 1), 16: chip(1, 1), 17: chip(2, 1),
    }

    def send(k, *tags):
        for t in tags:
            copy(k, t, *plan[t]).start()

    def wait(k, *tags):
        for t in tags:
            if t < 18:
                copy(k, t, came[t], plan[t][1], plan[t][2]).wait_recv()
            else:
                copy(k, t, plan[t][0], plan[t][1], plan[t][2], 1).wait_recv()

    def scale(k):
        e, here = c * CHUNKS + k, chip(0, 0)
        pltpu.make_async_copy(got.at[k, 0], got.at[k, 0], own_sem.at[k]).wait()
        pltpu.make_async_copy(got.at[k, pl.ds(0, SOURCES - 1)], got.at[k, pl.ds(0, SOURCES - 1)], in_sem.at[k]).wait()
        for j in range(SOURCES):
            rows[pl.ds(j * ROWS, ROWS), :] = got[k, j].astype(jnp.float32)
        row = lax.broadcasted_iota(jnp.int32, (16, QB), 0)
        scales = jnp.zeros((16, QB), jnp.float32)
        for b in range(BLOCKS):
            v = rows[pl.ds(b * QB, QB), :]
            m = jnp.max(jnp.max(jnp.abs(v), axis=0, keepdims=True), axis=1, keepdims=True) + 1e-06
            s = jnp.broadcast_to(m, (16, QB)).astype(jnp.bfloat16).astype(jnp.float32)
            buf[e, here, pl.ds(b * QB, QB), :] = (v / s[0:1]).astype(jnp.bfloat16)
            scales = jnp.where(row == b, s, scales)
        buf[e, here, pl.ds(SHARE, 16), :] = scales.astype(jnp.bfloat16)
        send(k, 0, 2, 4, 5, 1, 3, 6, 18)

    for step, k in ORDER:
        if step == "scale":
            scale(k)
        else:
            wait(k, *STEPS[step][0])
            send(k, *STEPS[step][1])
    for k in range(CHUNKS):
        for t in range(18, TAGS):
            wait(k, t)
        for t in range(TAGS):
            copy(k, t, *plan[t]).wait_send()
        pltpu.make_async_copy(got.at[k, pl.ds(0, SOURCES - 1)], got.at[k, pl.ds(0, SOURCES - 1)], out_sem.at[k]).wait()


def place(slot_ref, buf, out_ref, scale_ref, found, sem, scale_sem):
    for s in range(EXPERTS):
        e = slot_ref[s]
        for ch in range(CHIPS):
            pltpu.make_async_copy(
                buf.at[e, ch, pl.ds(0, SHARE)], out_ref.at[s, pl.ds(ch * SHARE, SHARE)], sem.at[s, ch]
            ).start()
    row = lax.broadcasted_iota(jnp.int32, (16, QB), 0)
    lane = lax.broadcasted_iota(jnp.int32, (16, QB), 1)
    lines = jnp.zeros((16, QB), jnp.float32)
    for s in range(EXPERTS):
        e = slot_ref[s]
        line = jnp.zeros((16, QB), jnp.float32)
        for ch in range(CHIPS):
            here = (lane - row == ch * BLOCKS) & (row < BLOCKS)
            line += jnp.where(here, buf[e, ch, pl.ds(SHARE, 16), :].astype(jnp.float32), 0.0)
        line = jnp.sum(line, axis=0, keepdims=True)
        lines = jnp.where(row == s, jnp.broadcast_to(line, (16, QB)), lines)
    found[...] = lines[:EXPERTS, : CHIPS * BLOCKS].astype(jnp.bfloat16)
    out = pltpu.make_async_copy(found, scale_ref, scale_sem)
    out.start()
    for s in range(EXPERTS):
        for ch in range(CHIPS):
            pltpu.make_async_copy(
                buf.at[0, ch, pl.ds(0, SHARE)], out_ref.at[s, pl.ds(ch * SHARE, SHARE)], sem.at[s, ch]
            ).wait()
    out.wait()


def shards(trainer_gate, expert_of_slot):
    gathered = pl.pallas_call(
        spread,
        out_shape=pltpu.VMEM((EXPERTS, CHIPS, FULL, QB), jnp.bfloat16),
        in_specs=[pl.BlockSpec(memory_space=pl.ANY)],
        out_specs=pl.BlockSpec(memory_space=pltpu.VMEM),
        scratch_shapes=[
            pltpu.VMEM((EXPERTS, ROWS, FF), jnp.bfloat16),
            pltpu.VMEM((CHUNKS, SOURCES, ROWS, QB), jnp.bfloat16),
            pltpu.VMEM((SHARE, QB), jnp.float32),
            pltpu.SemaphoreType.DMA,
            pltpu.SemaphoreType.DMA((CHUNKS,)),
            pltpu.SemaphoreType.DMA((CHUNKS,)),
            pltpu.SemaphoreType.DMA((CHUNKS,)),
            pltpu.SemaphoreType.DMA((CHUNKS, TAGS)),
            pltpu.SemaphoreType.DMA((CHUNKS, TAGS)),
        ],
        compiler_params=pltpu.CompilerParams(collective_id=0, has_side_effects=True, vmem_limit_bytes=52 * 2**20),
        name="spread",
    )(trainer_gate)
    placed, scales = pl.pallas_call(
        place,
        out_shape=(
            jax.ShapeDtypeStruct((EXPERTS, CHIPS * SHARE, QB), jnp.bfloat16),
            jax.ShapeDtypeStruct((EXPERTS, CHIPS * BLOCKS), jnp.bfloat16),
        ),
        in_specs=[pl.BlockSpec(memory_space=pltpu.SMEM), pl.BlockSpec(memory_space=pltpu.VMEM)],
        out_specs=(pl.BlockSpec(memory_space=pl.ANY), pl.BlockSpec(memory_space=pl.ANY)),
        scratch_shapes=[
            pltpu.VMEM((EXPERTS, CHIPS * BLOCKS), jnp.bfloat16),
            pltpu.SemaphoreType.DMA((EXPERTS, CHIPS)),
            pltpu.SemaphoreType.DMA,
        ],
        compiler_params=pltpu.CompilerParams(vmem_limit_bytes=20 * 2**20),
        name="place",
    )(expert_of_slot, gathered)
    return placed, scales.reshape(EXPERTS, CHIPS * BLOCKS, 1)


def solution(mesh):
    return jax.shard_map(
        shards,
        mesh=mesh,
        in_specs=(P(None, ("rep", "grp"), None), P()),
        out_specs=(P(None, None, "grp"), P(None, None, "grp")),
        check_vma=False,
    )
```

```python
import jax
import jax.numpy as jnp
from jax import lax
from jax.experimental import pallas as pl
from jax.experimental.pallas import tpu as pltpu
from jax.sharding import PartitionSpec as P

MESH = pl.DeviceIdType.MESH
EXPERTS, ROWS, FF = 6, 28, 2048
QB = 128
NX, NZ, NY, CORES = 4, 4, 4, 2
SHARE = 32 * ROWS
BLOCKS = SHARE // QB
CHIPS = 8
BATCHES = ((0, 4), (4, 2))
PIECE = (112, 64)

SAME, NEAR, AWAY = range(3)
CHUNKS = ((0, SAME), (0, NEAR), (0, AWAY), (1, SAME), (1, NEAR), (1, AWAY))
SOURCES = {SAME: 4, NEAR: 8, AWAY: 4}
ENDS = (208, 288, 112, 96, 144, 64)
TAGS = 32
H1, H2, A1, A2, MID, ALL = range(6)

(
    UP_1, DOWN_2, UP_ALL, DOWN_ALL, SIDE_1, SIDE_2,
    SIDE_ALL, FAR, UP_SIDE_1, DOWN_SIDE_2, UP_SIDE_2, DOWN_SIDE_1,
    UP_BETWEEN, DOWN_BETWEEN, FAR_BETWEEN, FAR_SIDE_1, FAR_SIDE_2,
) = range(17)
OWN, SCALE, ROUND = range(17, 20)
STEPS = {
    UP_1: ((0,), (7,)),
    DOWN_2: ((2,), (8,)),
    UP_ALL: ((1,), (15, 20)),
    DOWN_ALL: ((3,), (16, 21)),
    SIDE_1: ((4,), (9, 12)),
    SIDE_2: ((5,), (11, 10)),
    SIDE_ALL: ((6,), (19,)),
    FAR: ((7, 8), (17, 22)),
    UP_SIDE_1: ((9,), (13, 23)),
    DOWN_SIDE_2: ((11,), (14, 25)),
    UP_SIDE_2: ((10,), (24,)),
    DOWN_SIDE_1: ((12,), (26,)),
    UP_BETWEEN: ((15,), (29,)),
    DOWN_BETWEEN: ((16,), (30,)),
    FAR_BETWEEN: ((17,), (31,)),
    FAR_SIDE_1: ((13,), (27,)),
    FAR_SIDE_2: ((14,), (28,)),
}
FROM_TWIN = ((18, 19), (21, 25, 26, 30), (22, 27, 28, 31), (20, 23, 24, 29))
ORDER = (
    (ROUND, 0), (OWN, 0), (OWN, 3), (ROUND, 1), (ROUND, 2), (UP_1, 0), (DOWN_2, 0), (SIDE_1, 0), (UP_ALL, 0),
    (SIDE_2, 0), (DOWN_ALL, 0), (SIDE_ALL, 0), (UP_1, 3), (SIDE_1, 3), (DOWN_2, 3), (SIDE_2, 3), (UP_ALL, 3),
    (DOWN_ALL, 3), (SIDE_ALL, 3), (FAR, 0), (UP_SIDE_1, 0), (DOWN_SIDE_1, 0), (OWN, 1), (UP_SIDE_2, 0),
    (DOWN_SIDE_2, 0), (DOWN_SIDE_1, 3), (UP_SIDE_1, 3), (FAR, 3), (UP_SIDE_2, 3), (DOWN_SIDE_2, 3), (FAR_SIDE_1, 0),
    (UP_BETWEEN, 0), (DOWN_BETWEEN, 0), (UP_BETWEEN, 3), (OWN, 2), (DOWN_BETWEEN, 3), (DOWN_2, 1), (FAR_BETWEEN, 0),
    (UP_1, 1), (OWN, 4), (SIDE_1, 1), (DOWN_ALL, 1), (SIDE_2, 1), (UP_ALL, 1), (FAR_SIDE_2, 0), (FAR_SIDE_1, 3),
    (FAR_SIDE_2, 3), (SIDE_ALL, 1), (UP_1, 2), (DOWN_2, 2), (OWN, 5), (FAR_BETWEEN, 3), (SIDE_1, 2), (UP_ALL, 2),
    (DOWN_ALL, 2), (SIDE_2, 2), (SIDE_ALL, 2), (SIDE_1, 4), (FAR, 1), (SCALE, 0), (SIDE_2, 4), (UP_1, 4), (DOWN_2, 4),
    (SCALE, 1), (SIDE_ALL, 4), (UP_ALL, 4), (DOWN_ALL, 4), (DOWN_BETWEEN, 1), (UP_SIDE_1, 1), (DOWN_SIDE_1, 1),
    (UP_BETWEEN, 1), (SIDE_1, 5), (SIDE_2, 5), (UP_SIDE_2, 1), (DOWN_SIDE_2, 1), (SIDE_ALL, 5), (FAR, 2),
    (UP_BETWEEN, 2), (SCALE, 8), (UP_1, 5), (DOWN_2, 5), (SCALE, 9), (UP_ALL, 5), (DOWN_ALL, 5), (DOWN_BETWEEN, 2),
    (UP_SIDE_1, 2), (DOWN_SIDE_1, 2), (UP_SIDE_2, 2), (DOWN_SIDE_2, 2), (UP_SIDE_1, 4), (DOWN_SIDE_1, 4),
    (FAR_BETWEEN, 1), (SCALE, 6), (UP_SIDE_2, 4), (DOWN_SIDE_2, 4), (UP_BETWEEN, 4), (SCALE, 7), (FAR, 4),
    (DOWN_SIDE_1, 5), (DOWN_BETWEEN, 4), (DOWN_SIDE_2, 5), (SCALE, 2), (FAR_SIDE_1, 1), (FAR_BETWEEN, 2),
    (UP_SIDE_1, 5), (UP_SIDE_2, 5), (FAR_SIDE_2, 1), (UP_BETWEEN, 5), (SCALE, 3), (FAR, 5), (DOWN_BETWEEN, 5),
    (FAR_SIDE_1, 2), (SCALE, 14), (FAR_SIDE_2, 2), (SCALE, 15), (FAR_BETWEEN, 4), (FAR_SIDE_1, 4), (FAR_SIDE_2, 4),
    (FAR_SIDE_1, 5), (FAR_SIDE_2, 5), (SCALE, 10), (SCALE, 11), (FAR_BETWEEN, 5), (SCALE, 4), (SCALE, 5), (SCALE, 12),
    (SCALE, 13),
)


def spread(
    x_ref, buf, xv, stage0, stage1, raw0, raw1, rows, load_sem, own_sem, out_sem, in_sem, ready, ssem, rsem
):
    g, r = lax.axis_index("grp"), lax.axis_index("rep")
    x, zh = g // NZ, g % NZ
    y, z, c = r // 4, (r // 2) % 2, r % 2
    stage, raw = (stage0, stage1), (raw0, raw1)

    load = pltpu.make_async_copy(x_ref, xv, load_sem)
    load.start()

    def at(gx, gz, yy, zz, cc):
        return (gx % NX * NZ + gz % NZ, (yy % NY * 2 + zz) * 2 + cc)

    up, down = at(x, zh, y + 1, z, c), at(x, zh, y + 3, z, c)
    side, twin = at(x, zh, y, 1 - z, c), at(x, zh, y, z, 1 - c)
    out = at(x, zh + 3 + 2 * z, y, 1 - z, c)
    line = [at(x + d, zh, y, z, c) for d in (2, 1, 3)]
    near = line + [out, up, down, side, twin]

    def signal(sem, devices):
        for d in devices:
            pl.semaphore_signal(sem, inc=1, device_id=d, device_id_type=MESH)

    barrier = pltpu.get_barrier_semaphore()
    signal(barrier, near)

    load.wait()

    def pack(i, carry):
        col = pl.ds(pl.multiple_of(i * QB, QB), QB)
        for b, (first, count) in enumerate(BATCHES):
            for e in range(count):
                rows[0, pl.ds(e * ROWS, ROWS), :] = xv[first + e, :, col].astype(jnp.float32)
            stage[b][i] = rows[0, pl.ds(0, PIECE[b]), :].astype(jnp.bfloat16)
        return carry

    lax.fori_loop(0, NX * NZ, pack, 0)
    here = [pl.ds(pl.multiple_of((z * 4 + x) * n, 16), n) for n in PIECE]
    for b in range(2):
        pltpu.make_async_copy(stage[b].at[g], raw[b].at[y, c, zh, here[b]], own_sem.at[b]).start()

    def give(b, kind, gz, zz, dxs):
        for dx in dxs:
            pltpu.make_async_remote_copy(
                src_ref=stage[b].at[(x + dx) % NX * NZ + gz % NZ],
                dst_ref=raw[b].at[y, c, zh, here[b]],
                send_sem=out_sem.at[b, kind],
                recv_sem=in_sem.at[b, kind],
                device_id=at(x + dx, gz, y, zz, c),
                device_id_type=MESH,
            ).start()

    def region(k, chip):
        b, kind = CHUNKS[k]
        n = SOURCES[kind] * PIECE[b]
        if kind == SAME:
            return zh, chip[1] * n, n
        if kind == NEAR:
            return (zh + 3 + 2 * chip[1]) % NZ, 0, n
        return (zh + 2) % NZ, (1 - chip[1]) * n, n

    def part(k, chip, core, first, n):
        gz, base, _ = region(k, chip)
        return raw[CHUNKS[k][0]].at[chip[0], core, gz, pl.ds(pl.multiple_of(base + first, 16), n)]

    def chip(dy, dz):
        return ((y + dy) % NY, (z + dz) % 2)

    def pieces(k):
        n = SOURCES[CHUNKS[k][1]] * PIECE[CHUNKS[k][0]]
        a, h = ENDS[k], n // 2
        return {H1: (0, h), H2: (h, h), A1: (0, a), A2: (n - a, a), MID: (a, n - 2 * a), ALL: (0, n)}

    plan = {
        0: (chip(0, 0), H1, up),
        1: (chip(0, 0), H2, up),
        2: (chip(0, 0), H2, down),
        3: (chip(0, 0), H1, down),
        4: (chip(0, 0), A1, side),
        5: (chip(0, 0), A2, side),
        6: (chip(0, 0), MID, side),
        7: (chip(3, 0), H1, up),
        8: (chip(1, 0), H2, down),
        9: (chip(0, 1), A1, up),
        10: (chip(0, 1), A2, up),
        11: (chip(0, 1), A2, down),
        12: (chip(0, 1), A1, down),
        13: (chip(3, 1), A1, up),
        14: (chip(1, 1), A2, down),
        15: (chip(3, 0), MID, side),
        16: (chip(1, 0), MID, side),
        17: (chip(2, 0), MID, side),
        18: (chip(0, 0), ALL, twin),
        19: (chip(0, 1), ALL, twin),
        20: (chip(3, 0), ALL, twin),
        21: (chip(1, 0), ALL, twin),
        22: (chip(2, 0), ALL, twin),
        23: (chip(3, 1), A1, twin),
        24: (chip(3, 1), A2, twin),
        25: (chip(1, 1), A2, twin),
        26: (chip(1, 1), A1, twin),
        27: (chip(2, 1), A1, twin),
        28: (chip(2, 1), A2, twin),
        29: (chip(3, 1), MID, twin),
        30: (chip(1, 1), MID, twin),
        31: (chip(2, 1), MID, twin),
    }
    came = {
        0: chip(3, 0), 1: chip(3, 0), 2: chip(1, 0), 3: chip(1, 0),
        4: chip(0, 1), 5: chip(0, 1), 6: chip(0, 1),
        7: chip(2, 0), 8: chip(2, 0),
        9: chip(3, 1), 10: chip(3, 1), 11: chip(1, 1), 12: chip(1, 1),
        13: chip(2, 1), 14: chip(2, 1),
        15: chip(3, 1), 16: chip(1, 1), 17: chip(2, 1),
    }

    def copy(k, tag, origin, core):
        _, piece, target = plan[tag]
        ref = part(k, origin, core, *pieces(k)[piece])
        return pltpu.make_async_remote_copy(
            src_ref=ref,
            dst_ref=ref,
            send_sem=ssem.at[k, tag],
            recv_sem=rsem.at[k, tag],
            device_id=target,
            device_id_type=MESH,
        )

    def send(k, *tags):
        for t in tags:
            copy(k, t, plan[t][0], c).start()

    def wait(k, *tags):
        for t in tags:
            copy(k, t, came[t] if t < 18 else plan[t][0], c if t < 18 else 1 - c).wait_recv()

    def own(k):
        b, kind = CHUNKS[k]
        lot = 3 if kind == SAME else SOURCES[kind]
        if kind == SAME:
            pltpu.make_async_copy(stage[b].at[g], raw[b].at[y, c, zh, here[b]], own_sem.at[b]).wait()
        got = part(k, chip(0, 0), c, 0, lot * PIECE[b])
        pltpu.make_async_copy(got, got, in_sem.at[b, k % 3]).wait()
        send(k, 0, 2, 4, 5, 1, 3, 6, 18)

    def scale(b, dy, zs):
        if zs == 0:
            for k in range(3 * b, 3 * b + 3):
                wait(k, *FROM_TWIN[dy])
        first, count = BATCHES[b]
        n, ys = PIECE[b], (y + dy) % NY

        def fetch(i, carry):
            cc, xs = i // NX, i % NX
            at_row = pl.ds(pl.multiple_of((zs * 4 + xs) * n, 16), n)
            to = rows.at[:, pl.ds(pl.multiple_of(i * 4 * ROWS, 16), 4 * ROWS), :]
            for gz in range(NZ):
                v = raw[b][ys, cc, gz, at_row, :].astype(jnp.float32)
                for e in range(count):
                    to[e, pl.ds(gz * ROWS, ROWS), :] = v[e * ROWS : (e + 1) * ROWS]
            return carry

        lax.fori_loop(0, CORES * NX, fetch, 0)
        row = lax.broadcasted_iota(jnp.int32, (16, QB), 0)

        def expert(e, carry):
            found = jnp.zeros((16, QB), jnp.float32)
            for blk in range(BLOCKS):
                v = rows[e, pl.ds(blk * QB, QB), :]
                m = jnp.max(jnp.max(jnp.abs(v), axis=0, keepdims=True), axis=1, keepdims=True) + 1e-06
                s = jnp.broadcast_to(m, (16, QB)).astype(jnp.bfloat16).astype(jnp.float32)
                buf[first + e, ys * 2 + zs, pl.ds(blk * QB, QB), :] = (v / s[0:1]).astype(jnp.bfloat16)
                found = jnp.where(row == blk, s, found)
            buf[first + e, ys * 2 + zs, pl.ds(SHARE, 16), :] = found.astype(jnp.bfloat16)
            return carry

        lax.fori_loop(0, count, expert, 0)

    def further(i):
        pl.semaphore_wait(ready.at[i], len(line) + 2 if i == 0 else 2)
        if i < 2:
            signal(ready.at[i + 1], [side, out])
        if i == 0:
            give(0, NEAR, zh + 3 + 2 * z, 1 - z, (2, 1, 3, 0))
        elif i == 1:
            give(0, NEAR, zh + 1 + 2 * z, z, (2, 1, 3, 0))
        else:
            give(0, AWAY, zh + 2, 1 - z, (2, 1, 3, 0))
            give(1, NEAR, zh + 3 + 2 * z, 1 - z, (2, 1, 3, 0))
            give(1, NEAR, zh + 1 + 2 * z, z, (2, 1, 3, 0))
            give(1, AWAY, zh + 2, 1 - z, (2, 1, 3, 0))

    pl.semaphore_wait(barrier, len(near))
    signal(ready.at[0], line + [side, out])
    for b in range(2):
        give(b, SAME, zh, z, (2, 1, 3))

    for step, k in ORDER:
        if step == ROUND:
            further(k)
        elif step == OWN:
            own(k)
        elif step == SCALE:
            scale(k // 8, k // 2 % NY, k % 2)
        else:
            wait(k, *STEPS[step][0])
            send(k, *STEPS[step][1])

    for k, (b, kind) in enumerate(CHUNKS):
        for t in range(TAGS):
            copy(k, t, plan[t][0], c).wait_send()
        lot = 3 if kind == SAME else SOURCES[kind]
        gone = part(k, chip(0, 0), c, 0, lot * PIECE[b])
        pltpu.make_async_copy(gone, gone, out_sem.at[b, k % 3]).wait()


def place(slot_ref, buf, out_ref, scale_ref, found, sem, scale_sem):
    for s in range(EXPERTS):
        e = slot_ref[s]
        for ch in range(CHIPS):
            pltpu.make_async_copy(
                buf.at[e, ch, pl.ds(0, SHARE)], out_ref.at[s, pl.ds(ch * SHARE, SHARE)], sem.at[s, ch]
            ).start()
    row = lax.broadcasted_iota(jnp.int32, (16, QB), 0)
    lane = lax.broadcasted_iota(jnp.int32, (16, QB), 1)
    lines = jnp.zeros((16, QB), jnp.float32)
    for s in range(EXPERTS):
        e = slot_ref[s]
        line = jnp.zeros((16, QB), jnp.float32)
        for ch in range(CHIPS):
            here = (lane - row == ch * BLOCKS) & (row < BLOCKS)
            line += jnp.where(here, buf[e, ch, pl.ds(SHARE, 16), :].astype(jnp.float32), 0.0)
        line = jnp.sum(line, axis=0, keepdims=True)
        lines = jnp.where(row == s, jnp.broadcast_to(line, (16, QB)), lines)
    found[...] = lines[:EXPERTS, : CHIPS * BLOCKS].astype(jnp.bfloat16)
    out = pltpu.make_async_copy(found, scale_ref, scale_sem)
    out.start()
    for s in range(EXPERTS):
        for ch in range(CHIPS):
            pltpu.make_async_copy(
                buf.at[0, ch, pl.ds(0, SHARE)], out_ref.at[s, pl.ds(ch * SHARE, SHARE)], sem.at[s, ch]
            ).wait()
    out.wait()


def shards(trainer_gate, expert_of_slot):
    rest = [pltpu.VMEM((NY, CORES, NZ, 8 * n, QB), jnp.bfloat16) for n in PIECE]
    ready_to_go = [pltpu.VMEM((NX * NZ, n, QB), jnp.bfloat16) for n in PIECE]
    gathered = pl.pallas_call(
        spread,
        out_shape=pltpu.VMEM((EXPERTS, CHIPS, SHARE + 16, QB), jnp.bfloat16),
        in_specs=[pl.BlockSpec(memory_space=pl.ANY)],
        out_specs=pl.BlockSpec(memory_space=pltpu.VMEM),
        scratch_shapes=[
            pltpu.VMEM((EXPERTS, ROWS, FF), jnp.bfloat16),
            *ready_to_go,
            *rest,
            pltpu.VMEM((4, SHARE, QB), jnp.float32),
            pltpu.SemaphoreType.DMA,
            pltpu.SemaphoreType.DMA((2,)),
            pltpu.SemaphoreType.DMA((2, 3)),
            pltpu.SemaphoreType.DMA((2, 3)),
            pltpu.SemaphoreType.REGULAR((3,)),
            pltpu.SemaphoreType.DMA((len(CHUNKS), TAGS)),
            pltpu.SemaphoreType.DMA((len(CHUNKS), TAGS)),
        ],
        compiler_params=pltpu.CompilerParams(collective_id=0, has_side_effects=True, vmem_limit_bytes=52 * 2**20),
        name="spread",
    )(trainer_gate)
    placed, scales = pl.pallas_call(
        place,
        out_shape=(
            jax.ShapeDtypeStruct((EXPERTS, CHIPS * SHARE, QB), jnp.bfloat16),
            jax.ShapeDtypeStruct((EXPERTS, CHIPS * BLOCKS), jnp.bfloat16),
        ),
        in_specs=[
            pl.BlockSpec(memory_space=pltpu.SMEM),
            pl.BlockSpec(memory_space=pltpu.VMEM),
        ],
        out_specs=(pl.BlockSpec(memory_space=pl.ANY), pl.BlockSpec(memory_space=pl.ANY)),
        scratch_shapes=[
            pltpu.VMEM((EXPERTS, CHIPS * BLOCKS), jnp.bfloat16),
            pltpu.SemaphoreType.DMA((EXPERTS, CHIPS)),
            pltpu.SemaphoreType.DMA,
        ],
        compiler_params=pltpu.CompilerParams(vmem_limit_bytes=20 * 2**20),
        name="place",
    )(expert_of_slot, gathered)
    return placed, scales.reshape(EXPERTS, CHIPS * BLOCKS, 1)


def solution(mesh):
    return jax.shard_map(
        shards,
        mesh=mesh,
        in_specs=(P(None, ("rep", "grp"), None), P()),
        out_specs=(P(None, None, "grp"), P(None, None, "grp")),
        check_vma=False,
    )
```

```python
import jax
import jax.numpy as jnp
from jax import lax
from jax.experimental import pallas as pl
from jax.experimental.pallas import tpu as pltpu
from jax.sharding import PartitionSpec as P

MESH = pl.DeviceIdType.MESH
EXPERTS, ROWS, FF = 6, 28, 2048
QB = 128
NX, NZ, NY, CORES = 4, 4, 4, 2
SHARE = 32 * ROWS
BLOCKS = SHARE // QB
CHIPS = 8
BATCHES = ((0, 4), (4, 2))
PIECE = (112, 64)

SAME, NEAR, AWAY = range(3)
CHUNKS = ((0, SAME), (0, NEAR), (0, AWAY), (1, SAME), (1, NEAR), (1, AWAY))
SOURCES = {SAME: 4, NEAR: 8, AWAY: 4}
ENDS = (208, 256, 128, 112, 112, 80)
TAGS = 32
H1, H2, A1, A2, MID, ALL = range(6)

(
    UP_1, DOWN_2, UP_ALL, DOWN_ALL, SIDE_1, SIDE_2,
    SIDE_ALL, FAR, UP_SIDE_1, DOWN_SIDE_2, UP_SIDE_2, DOWN_SIDE_1,
    UP_BETWEEN, DOWN_BETWEEN, FAR_BETWEEN, FAR_SIDE_1, FAR_SIDE_2,
) = range(17)
OWN, SCALE, ROUND = range(17, 20)
STEPS = {
    UP_1: ((0,), (7,)),
    DOWN_2: ((2,), (8,)),
    UP_ALL: ((1,), (15, 20)),
    DOWN_ALL: ((3,), (16, 21)),
    SIDE_1: ((4,), (9, 12)),
    SIDE_2: ((5,), (11, 10)),
    SIDE_ALL: ((6,), (19,)),
    FAR: ((7, 8), (17, 22)),
    UP_SIDE_1: ((9,), (13, 23)),
    DOWN_SIDE_2: ((11,), (14, 25)),
    UP_SIDE_2: ((10,), (24,)),
    DOWN_SIDE_1: ((12,), (26,)),
    UP_BETWEEN: ((15,), (29,)),
    DOWN_BETWEEN: ((16,), (30,)),
    FAR_BETWEEN: ((17,), (31,)),
    FAR_SIDE_1: ((13,), (27,)),
    FAR_SIDE_2: ((14,), (28,)),
}
FROM_TWIN = ((18, 19), (21, 25, 26, 30), (22, 27, 28, 31), (20, 23, 24, 29))
WHOLE = (0, 1, 2, 3, 4, )
WHOLE_STEPS = {
    **STEPS,
    UP_SIDE_1: ((9,), (13,)),
    DOWN_SIDE_2: ((11,), (14,)),
    UP_SIDE_2: ((10, 15), (23,)),
    DOWN_SIDE_1: ((12, 16), (25,)),
    FAR_SIDE_1: ((13, 14, 17), (27,)),
}
WHOLE_FROM_TWIN = ((18, 19), (21, 25), (22, 27), (20, 23))
ORDER = (
    (ROUND, 0), (OWN, 0), (OWN, 3), (ROUND, 1), (ROUND, 2), (UP_1, 0), (DOWN_2, 0), (SIDE_1, 0), (UP_ALL, 0),
    (SIDE_2, 0), (DOWN_ALL, 0), (SIDE_ALL, 0), (UP_1, 3), (DOWN_2, 3), (SIDE_1, 3), (UP_ALL, 3), (SIDE_2, 3),
    (DOWN_ALL, 3), (SIDE_ALL, 3), (FAR, 0), (UP_SIDE_1, 0), (OWN, 1), (DOWN_SIDE_2, 0), (FAR, 3), (UP_SIDE_1, 3),
    (DOWN_SIDE_2, 3), (UP_SIDE_2, 0), (DOWN_SIDE_1, 0), (UP_SIDE_2, 3), (DOWN_SIDE_1, 3), (OWN, 2), (DOWN_2, 1),
    (SIDE_1, 1), (UP_1, 1), (OWN, 4), (SIDE_2, 1), (DOWN_ALL, 1), (UP_ALL, 1), (FAR_SIDE_1, 0), (SIDE_ALL, 1),
    (FAR_SIDE_1, 3), (OWN, 5), (UP_1, 2), (SIDE_1, 2), (DOWN_2, 2), (SIDE_2, 2), (UP_ALL, 2), (DOWN_ALL, 2),
    (SIDE_ALL, 2), (SIDE_1, 4), (UP_SIDE_1, 1), (SIDE_2, 4), (SCALE, 0), (SCALE, 1), (SIDE_ALL, 4), (FAR, 1),
    (UP_1, 4), (DOWN_2, 4), (UP_ALL, 4), (DOWN_ALL, 4), (SIDE_1, 5), (UP_SIDE_2, 1), (DOWN_SIDE_2, 1),
    (DOWN_SIDE_1, 1), (SIDE_2, 5), (UP_1, 5), (DOWN_2, 5), (SIDE_ALL, 5), (UP_ALL, 5), (DOWN_ALL, 5), (SCALE, 8),
    (SCALE, 9), (UP_SIDE_1, 2), (FAR, 2), (UP_SIDE_2, 2), (DOWN_SIDE_2, 2), (DOWN_SIDE_1, 2), (UP_SIDE_1, 4),
    (DOWN_SIDE_2, 4), (SCALE, 6), (SCALE, 7), (UP_SIDE_2, 4), (DOWN_SIDE_1, 5), (SCALE, 2), (FAR, 4),
    (DOWN_SIDE_1, 4), (UP_SIDE_1, 5), (FAR_SIDE_1, 1), (UP_BETWEEN, 5), (UP_SIDE_2, 5), (DOWN_SIDE_2, 5), (SCALE, 3),
    (DOWN_BETWEEN, 5), (FAR, 5), (FAR_SIDE_1, 2), (SCALE, 14), (SCALE, 15), (SCALE, 10), (FAR_SIDE_1, 5),
    (FAR_SIDE_2, 5), (SCALE, 11), (FAR_SIDE_1, 4), (FAR_BETWEEN, 5), (SCALE, 4), (SCALE, 5), (SCALE, 12), (SCALE, 13),
)


def spread(
    x_ref, buf, xv, stage0, stage1, raw0, raw1, rows, load_sem, own_sem, out_sem, in_sem, ready, ssem, rsem
):
    g, r = lax.axis_index("grp"), lax.axis_index("rep")
    x, zh = g // NZ, g % NZ
    y, z, c = r // 4, (r // 2) % 2, r % 2
    stage, raw = (stage0, stage1), (raw0, raw1)

    load = pltpu.make_async_copy(x_ref, xv, load_sem)
    load.start()

    def at(gx, gz, yy, zz, cc):
        return (gx % NX * NZ + gz % NZ, (yy % NY * 2 + zz) * 2 + cc)

    up, down = at(x, zh, y + 1, z, c), at(x, zh, y + 3, z, c)
    side, twin = at(x, zh, y, 1 - z, c), at(x, zh, y, z, 1 - c)
    out = at(x, zh + 3 + 2 * z, y, 1 - z, c)
    line = [at(x + d, zh, y, z, c) for d in (2, 1, 3)]
    near = line + [out, up, down, side, twin]

    def signal(sem, devices):
        for d in devices:
            pl.semaphore_signal(sem, inc=1, device_id=d, device_id_type=MESH)

    barrier = pltpu.get_barrier_semaphore()
    signal(barrier, near)

    load.wait()

    def pack(i, carry):
        col = pl.ds(pl.multiple_of(i * QB, QB), QB)
        for b, (first, count) in enumerate(BATCHES):
            for e in range(count):
                rows[0, pl.ds(e * ROWS, ROWS), :] = xv[first + e, :, col].astype(jnp.float32)
            stage[b][i] = rows[0, pl.ds(0, PIECE[b]), :].astype(jnp.bfloat16)
        return carry

    lax.fori_loop(0, NX * NZ, pack, 0)
    here = [pl.ds(pl.multiple_of((z * 4 + x) * n, 16), n) for n in PIECE]
    for b in range(2):
        pltpu.make_async_copy(stage[b].at[g], raw[b].at[y, c, zh, here[b]], own_sem.at[b]).start()

    def give(b, kind, gz, zz, dxs):
        for dx in dxs:
            pltpu.make_async_remote_copy(
                src_ref=stage[b].at[(x + dx) % NX * NZ + gz % NZ],
                dst_ref=raw[b].at[y, c, zh, here[b]],
                send_sem=out_sem.at[b, kind],
                recv_sem=in_sem.at[b, kind],
                device_id=at(x + dx, gz, y, zz, c),
                device_id_type=MESH,
            ).start()

    def region(k, chip):
        b, kind = CHUNKS[k]
        n = SOURCES[kind] * PIECE[b]
        if kind == SAME:
            return zh, chip[1] * n, n
        if kind == NEAR:
            return (zh + 3 + 2 * chip[1]) % NZ, 0, n
        return (zh + 2) % NZ, (1 - chip[1]) * n, n

    def part(k, chip, core, first, n):
        gz, base, _ = region(k, chip)
        return raw[CHUNKS[k][0]].at[chip[0], core, gz, pl.ds(pl.multiple_of(base + first, 16), n)]

    def chip(dy, dz):
        return ((y + dy) % NY, (z + dz) % 2)

    def pieces(k):
        n = SOURCES[CHUNKS[k][1]] * PIECE[CHUNKS[k][0]]
        a, h = ENDS[k], n // 2
        return {H1: (0, h), H2: (h, h), A1: (0, a), A2: (n - a, a), MID: (a, n - 2 * a), ALL: (0, n)}

    plan = {
        0: (chip(0, 0), H1, up),
        1: (chip(0, 0), H2, up),
        2: (chip(0, 0), H2, down),
        3: (chip(0, 0), H1, down),
        4: (chip(0, 0), A1, side),
        5: (chip(0, 0), A2, side),
        6: (chip(0, 0), MID, side),
        7: (chip(3, 0), H1, up),
        8: (chip(1, 0), H2, down),
        9: (chip(0, 1), A1, up),
        10: (chip(0, 1), A2, up),
        11: (chip(0, 1), A2, down),
        12: (chip(0, 1), A1, down),
        13: (chip(3, 1), A1, up),
        14: (chip(1, 1), A2, down),
        15: (chip(3, 0), MID, side),
        16: (chip(1, 0), MID, side),
        17: (chip(2, 0), MID, side),
        18: (chip(0, 0), ALL, twin),
        19: (chip(0, 1), ALL, twin),
        20: (chip(3, 0), ALL, twin),
        21: (chip(1, 0), ALL, twin),
        22: (chip(2, 0), ALL, twin),
        23: (chip(3, 1), A1, twin),
        24: (chip(3, 1), A2, twin),
        25: (chip(1, 1), A2, twin),
        26: (chip(1, 1), A1, twin),
        27: (chip(2, 1), A1, twin),
        28: (chip(2, 1), A2, twin),
        29: (chip(3, 1), MID, twin),
        30: (chip(1, 1), MID, twin),
        31: (chip(2, 1), MID, twin),
    }
    came = {
        0: chip(3, 0), 1: chip(3, 0), 2: chip(1, 0), 3: chip(1, 0),
        4: chip(0, 1), 5: chip(0, 1), 6: chip(0, 1),
        7: chip(2, 0), 8: chip(2, 0),
        9: chip(3, 1), 10: chip(3, 1), 11: chip(1, 1), 12: chip(1, 1),
        13: chip(2, 1), 14: chip(2, 1),
        15: chip(3, 1), 16: chip(1, 1), 17: chip(2, 1),
    }

    def copy(k, tag, origin, core):
        _, piece, target = plan[tag]
        if k in WHOLE and tag > 22:
            piece = ALL
        ref = part(k, origin, core, *pieces(k)[piece])
        return pltpu.make_async_remote_copy(
            src_ref=ref,
            dst_ref=ref,
            send_sem=ssem.at[k, tag],
            recv_sem=rsem.at[k, tag],
            device_id=target,
            device_id_type=MESH,
        )

    def send(k, *tags):
        for t in tags:
            copy(k, t, plan[t][0], c).start()

    def wait(k, *tags):
        for t in tags:
            copy(k, t, came[t] if t < 18 else plan[t][0], c if t < 18 else 1 - c).wait_recv()

    def own(k):
        b, kind = CHUNKS[k]
        lot = 3 if kind == SAME else SOURCES[kind]
        if kind == SAME:
            pltpu.make_async_copy(stage[b].at[g], raw[b].at[y, c, zh, here[b]], own_sem.at[b]).wait()
        got = part(k, chip(0, 0), c, 0, lot * PIECE[b])
        pltpu.make_async_copy(got, got, in_sem.at[b, k % 3]).wait()
        send(k, 0, 2, 4, 5, 1, 3, 6, 18)

    def scale(b, dy, zs):
        if zs == 0:
            for k in range(3 * b, 3 * b + 3):
                wait(k, *(WHOLE_FROM_TWIN if k in WHOLE else FROM_TWIN)[dy])
        first, count = BATCHES[b]
        n, ys = PIECE[b], (y + dy) % NY

        def fetch(i, carry):
            cc, xs = i // NX, i % NX
            at_row = pl.ds(pl.multiple_of((zs * 4 + xs) * n, 16), n)
            to = rows.at[:, pl.ds(pl.multiple_of(i * 4 * ROWS, 16), 4 * ROWS), :]
            for gz in range(NZ):
                v = raw[b][ys, cc, gz, at_row, :].astype(jnp.float32)
                for e in range(count):
                    to[e, pl.ds(gz * ROWS, ROWS), :] = v[e * ROWS : (e + 1) * ROWS]
            return carry

        lax.fori_loop(0, CORES * NX, fetch, 0)
        row = lax.broadcasted_iota(jnp.int32, (16, QB), 0)

        def expert(e, carry):
            found = jnp.zeros((16, QB), jnp.float32)
            for blk in range(BLOCKS):
                v = rows[e, pl.ds(blk * QB, QB), :]
                m = jnp.max(jnp.max(jnp.abs(v), axis=0, keepdims=True), axis=1, keepdims=True) + 1e-06
                s = jnp.broadcast_to(m, (16, QB)).astype(jnp.bfloat16).astype(jnp.float32)
                buf[first + e, ys * 2 + zs, pl.ds(blk * QB, QB), :] = (v / s[0:1]).astype(jnp.bfloat16)
                found = jnp.where(row == blk, s, found)
            buf[first + e, ys * 2 + zs, pl.ds(SHARE, 16), :] = found.astype(jnp.bfloat16)
            return carry

        lax.fori_loop(0, count, expert, 0)

    def further(i):
        pl.semaphore_wait(ready.at[i], len(line) + 2 if i == 0 else 2)
        if i < 2:
            signal(ready.at[i + 1], [side, out])
        if i == 0:
            give(0, NEAR, zh + 3 + 2 * z, 1 - z, (2, 1, 3, 0))
        elif i == 1:
            give(0, NEAR, zh + 1 + 2 * z, z, (2, 1, 3, 0))
        else:
            give(0, AWAY, zh + 2, 1 - z, (2, 1, 3, 0))
            give(1, NEAR, zh + 3 + 2 * z, 1 - z, (2, 1, 3, 0))
            give(1, NEAR, zh + 1 + 2 * z, z, (2, 1, 3, 0))
            give(1, AWAY, zh + 2, 1 - z, (2, 1, 3, 0))

    pl.semaphore_wait(barrier, len(near))
    signal(ready.at[0], line + [side, out])
    for b in range(2):
        give(b, SAME, zh, z, (2, 1, 3))

    for step, k in ORDER:
        if step == ROUND:
            further(k)
        elif step == OWN:
            own(k)
        elif step == SCALE:
            scale(k // 8, k // 2 % NY, k % 2)
        else:
            first, then = (WHOLE_STEPS if k in WHOLE else STEPS)[step]
            wait(k, *first)
            send(k, *then)

    for k, (b, kind) in enumerate(CHUNKS):
        for t in range(TAGS):
            if k not in WHOLE or t < 23 or t in (23, 25, 27):
                copy(k, t, plan[t][0], c).wait_send()
        lot = 3 if kind == SAME else SOURCES[kind]
        gone = part(k, chip(0, 0), c, 0, lot * PIECE[b])
        pltpu.make_async_copy(gone, gone, out_sem.at[b, k % 3]).wait()


def place(slot_ref, buf, out_ref, scale_ref, found, sem, scale_sem):
    for s in range(EXPERTS):
        e = slot_ref[s]
        pltpu.make_async_copy(buf.at[e, :, pl.ds(0, SHARE)], out_ref.at[s], sem.at[s]).start()
    row = lax.broadcasted_iota(jnp.int32, (16, QB), 0)
    lane = lax.broadcasted_iota(jnp.int32, (16, QB), 1)
    lines = jnp.zeros((16, QB), jnp.float32)
    for s in range(EXPERTS):
        e = slot_ref[s]
        line = jnp.zeros((16, QB), jnp.float32)
        for ch in range(CHIPS):
            here = (lane - row == ch * BLOCKS) & (row < BLOCKS)
            line += jnp.where(here, buf[e, ch, pl.ds(SHARE, 16), :].astype(jnp.float32), 0.0)
        line = jnp.sum(line, axis=0, keepdims=True)
        lines = jnp.where(row == s, jnp.broadcast_to(line, (16, QB)), lines)
    found[...] = lines[:EXPERTS, : CHIPS * BLOCKS].astype(jnp.bfloat16)
    out = pltpu.make_async_copy(found, scale_ref, scale_sem)
    out.start()
    for s in range(EXPERTS):
        pltpu.make_async_copy(buf.at[0, :, pl.ds(0, SHARE)], out_ref.at[s], sem.at[s]).wait()
    out.wait()


def shards(trainer_gate, expert_of_slot):
    rest = [pltpu.VMEM((NY, CORES, NZ, 8 * n, QB), jnp.bfloat16) for n in PIECE]
    ready_to_go = [pltpu.VMEM((NX * NZ, n, QB), jnp.bfloat16) for n in PIECE]
    gathered = pl.pallas_call(
        spread,
        out_shape=pltpu.VMEM((EXPERTS, CHIPS, SHARE + 16, QB), jnp.bfloat16),
        in_specs=[pl.BlockSpec(memory_space=pl.ANY)],
        out_specs=pl.BlockSpec(memory_space=pltpu.VMEM),
        scratch_shapes=[
            pltpu.VMEM((EXPERTS, ROWS, FF), jnp.bfloat16),
            *ready_to_go,
            *rest,
            pltpu.VMEM((4, SHARE, QB), jnp.float32),
            pltpu.SemaphoreType.DMA,
            pltpu.SemaphoreType.DMA((2,)),
            pltpu.SemaphoreType.DMA((2, 3)),
            pltpu.SemaphoreType.DMA((2, 3)),
            pltpu.SemaphoreType.REGULAR((3,)),
            pltpu.SemaphoreType.DMA((len(CHUNKS), TAGS)),
            pltpu.SemaphoreType.DMA((len(CHUNKS), TAGS)),
        ],
        compiler_params=pltpu.CompilerParams(collective_id=0, has_side_effects=True, vmem_limit_bytes=52 * 2**20),
        name="spread",
    )(trainer_gate)
    placed, scales = pl.pallas_call(
        place,
        out_shape=(
            jax.ShapeDtypeStruct((EXPERTS, CHIPS, SHARE, QB), jnp.bfloat16),
            jax.ShapeDtypeStruct((EXPERTS, CHIPS * BLOCKS), jnp.bfloat16),
        ),
        in_specs=[
            pl.BlockSpec(memory_space=pltpu.SMEM),
            pl.BlockSpec(memory_space=pltpu.VMEM),
        ],
        out_specs=(pl.BlockSpec(memory_space=pl.ANY), pl.BlockSpec(memory_space=pl.ANY)),
        scratch_shapes=[
            pltpu.VMEM((EXPERTS, CHIPS * BLOCKS), jnp.bfloat16),
            pltpu.SemaphoreType.DMA((EXPERTS,)),
            pltpu.SemaphoreType.DMA,
        ],
        compiler_params=pltpu.CompilerParams(vmem_limit_bytes=20 * 2**20),
        name="place",
    )(expert_of_slot, gathered)
    return placed.reshape(EXPERTS, CHIPS * SHARE, QB), scales.reshape(EXPERTS, CHIPS * BLOCKS, 1)


def solution(mesh):
    return jax.shard_map(
        shards,
        mesh=mesh,
        in_specs=(P(None, ("rep", "grp"), None), P()),
        out_specs=(P(None, None, "grp"), P(None, None, "grp")),
        check_vma=False,
    )
```

```python
import jax
import jax.numpy as jnp
from jax import lax
from jax.experimental import pallas as pl
from jax.experimental.pallas import tpu as pltpu
from jax.sharding import PartitionSpec as P

MESH = pl.DeviceIdType.MESH
EXPERTS, ROWS, FF = 6, 28, 2048
QB = 128
NX, NZ, NY, CORES = 4, 4, 4, 2
SHARE = 32 * ROWS
BLOCKS = SHARE // QB
CHIPS = 8
BATCHES = ((0, 4), (4, 2))
PIECE = (112, 64)

SAME, NEAR, AWAY = range(3)
CHUNKS = ((0, SAME), (0, NEAR), (0, AWAY), (1, SAME), (1, NEAR), (1, AWAY))
SOURCES = {SAME: 4, NEAR: 8, AWAY: 4}
ENDS = (208, 256, 128, 112, 112, 80)
TAGS = 32
H1, H2, A1, A2, MID, ALL = range(6)

(
    UP_1, DOWN_2, UP_ALL, DOWN_ALL, SIDE_1, SIDE_2,
    SIDE_ALL, FAR, UP_SIDE_1, DOWN_SIDE_2, UP_SIDE_2, DOWN_SIDE_1,
    UP_BETWEEN, DOWN_BETWEEN, FAR_BETWEEN, FAR_SIDE_1, FAR_SIDE_2,
) = range(17)
OWN, SCALE, ROUND = range(17, 20)
STEPS = {
    UP_1: ((0,), (7,)),
    DOWN_2: ((2,), (8,)),
    UP_ALL: ((1,), (15, 20)),
    DOWN_ALL: ((3,), (16, 21)),
    SIDE_1: ((4,), (9, 12)),
    SIDE_2: ((5,), (11, 10)),
    SIDE_ALL: ((6,), (19,)),
    FAR: ((7, 8), (17, 22)),
    UP_SIDE_1: ((9,), (13, 23)),
    DOWN_SIDE_2: ((11,), (14, 25)),
    UP_SIDE_2: ((10,), (24,)),
    DOWN_SIDE_1: ((12,), (26,)),
    UP_BETWEEN: ((15,), (29,)),
    DOWN_BETWEEN: ((16,), (30,)),
    FAR_BETWEEN: ((17,), (31,)),
    FAR_SIDE_1: ((13,), (27,)),
    FAR_SIDE_2: ((14,), (28,)),
}
FROM_TWIN = ((18, 19), (21, 25, 26, 30), (22, 27, 28, 31), (20, 23, 24, 29))
WHOLE = (0, 1, 2, 3, 4, )
WHOLE_STEPS = {
    **STEPS,
    UP_SIDE_1: ((9,), (13,)),
    DOWN_SIDE_2: ((11,), (14,)),
    UP_SIDE_2: ((10, 15), (23,)),
    DOWN_SIDE_1: ((12, 16), (25,)),
    FAR_SIDE_1: ((13, 14, 17), (27,)),
}
WHOLE_FROM_TWIN = ((18, 19), (21, 25), (22, 27), (20, 23))
ORDER = (
    (ROUND, 0), (OWN, 0), (ROUND, 1), (OWN, 3), (ROUND, 2), (UP_1, 0), (DOWN_2, 0), (SIDE_1, 0), (UP_ALL, 0),
    (SIDE_2, 0), (DOWN_ALL, 0), (SIDE_ALL, 0), (UP_1, 3), (DOWN_2, 3), (SIDE_1, 3), (UP_ALL, 3), (SIDE_2, 3),
    (DOWN_ALL, 3), (SIDE_ALL, 3), (FAR, 0), (UP_SIDE_1, 0), (OWN, 1), (DOWN_SIDE_2, 0), (FAR, 3), (UP_SIDE_1, 3),
    (DOWN_SIDE_2, 3), (UP_SIDE_2, 0), (DOWN_SIDE_1, 0), (UP_SIDE_2, 3), (DOWN_SIDE_1, 3), (OWN, 2), (DOWN_2, 1),
    (SIDE_1, 1), (UP_1, 1), (OWN, 4), (SIDE_2, 1), (DOWN_ALL, 1), (UP_ALL, 1), (FAR_SIDE_1, 0), (SIDE_ALL, 1),
    (FAR_SIDE_1, 3), (OWN, 5), (UP_1, 2), (SIDE_1, 2), (DOWN_2, 2), (SIDE_2, 2), (UP_ALL, 2), (DOWN_ALL, 2),
    (SIDE_ALL, 2), (SIDE_1, 4), (UP_SIDE_1, 1), (SIDE_2, 4), (SCALE, 0), (SCALE, 1), (SIDE_ALL, 4), (FAR, 1),
    (UP_1, 4), (DOWN_2, 4), (UP_ALL, 4), (DOWN_ALL, 4), (SIDE_1, 5), (UP_SIDE_2, 1), (DOWN_SIDE_2, 1),
    (DOWN_SIDE_1, 1), (SIDE_2, 5), (UP_1, 5), (DOWN_2, 5), (SIDE_ALL, 5), (UP_ALL, 5), (DOWN_ALL, 5), (SCALE, 8),
    (SCALE, 9), (UP_SIDE_1, 2), (FAR, 2), (UP_SIDE_2, 2), (DOWN_SIDE_2, 2), (DOWN_SIDE_1, 2), (UP_SIDE_1, 4),
    (DOWN_SIDE_2, 4), (SCALE, 6), (SCALE, 7), (UP_SIDE_2, 4), (DOWN_SIDE_1, 5), (SCALE, 2), (FAR, 4),
    (DOWN_SIDE_1, 4), (UP_SIDE_1, 5), (FAR_SIDE_1, 1), (UP_BETWEEN, 5), (UP_SIDE_2, 5), (DOWN_SIDE_2, 5), (SCALE, 3),
    (DOWN_BETWEEN, 5), (FAR, 5), (FAR_SIDE_1, 2), (SCALE, 14), (SCALE, 15), (SCALE, 10), (FAR_SIDE_1, 5),
    (FAR_SIDE_2, 5), (SCALE, 11), (FAR_SIDE_1, 4), (FAR_BETWEEN, 5), (SCALE, 4), (SCALE, 5), (SCALE, 12), (SCALE, 13),
)


def spread(
    x_ref, buf, xv, stage0, stage1, raw0, raw1, rows, load_sem, own_sem, out_sem, in_sem, ready, ssem, rsem
):
    g, r = lax.axis_index("grp"), lax.axis_index("rep")
    x, zh = g // NZ, g % NZ
    y, z, c = r // 4, (r // 2) % 2, r % 2
    stage, raw = (stage0, stage1), (raw0, raw1)

    load = pltpu.make_async_copy(x_ref, xv, load_sem)
    load.start()

    def at(gx, gz, yy, zz, cc):
        return (gx % NX * NZ + gz % NZ, (yy % NY * 2 + zz) * 2 + cc)

    up, down = at(x, zh, y + 1, z, c), at(x, zh, y + 3, z, c)
    side, twin = at(x, zh, y, 1 - z, c), at(x, zh, y, z, 1 - c)
    out = at(x, zh + 3 + 2 * z, y, 1 - z, c)
    line = [at(x + d, zh, y, z, c) for d in (2, 1, 3)]
    near = line + [out, up, down, side, twin]

    def signal(sem, devices):
        for d in devices:
            pl.semaphore_signal(sem, inc=1, device_id=d, device_id_type=MESH)

    barrier = pltpu.get_barrier_semaphore()
    signal(barrier, near)

    load.wait()

    def pack(i, carry):
        col = pl.ds(pl.multiple_of(i * QB, QB), QB)
        for b, (first, count) in enumerate(BATCHES):
            for e in range(count):
                rows[0, pl.ds(e * ROWS, ROWS), :] = xv[first + e, :, col].astype(jnp.float32)
            stage[b][i] = rows[0, pl.ds(0, PIECE[b]), :].astype(jnp.bfloat16)
        return carry

    lax.fori_loop(0, NX * NZ, pack, 0)
    here = [pl.ds(pl.multiple_of((z * 4 + x) * n, 16), n) for n in PIECE]
    for b in range(2):
        pltpu.make_async_copy(stage[b].at[g], raw[b].at[y, c, zh, here[b]], own_sem.at[b]).start()

    def give(b, kind, gz, zz, dxs):
        for dx in dxs:
            pltpu.make_async_remote_copy(
                src_ref=stage[b].at[(x + dx) % NX * NZ + gz % NZ],
                dst_ref=raw[b].at[y, c, zh, here[b]],
                send_sem=out_sem.at[b, kind],
                recv_sem=in_sem.at[b, kind],
                device_id=at(x + dx, gz, y, zz, c),
                device_id_type=MESH,
            ).start()

    def region(k, chip):
        b, kind = CHUNKS[k]
        n = SOURCES[kind] * PIECE[b]
        if kind == SAME:
            return zh, chip[1] * n, n
        if kind == NEAR:
            return (zh + 3 + 2 * chip[1]) % NZ, 0, n
        return (zh + 2) % NZ, (1 - chip[1]) * n, n

    def part(k, chip, core, first, n):
        gz, base, _ = region(k, chip)
        return raw[CHUNKS[k][0]].at[chip[0], core, gz, pl.ds(pl.multiple_of(base + first, 16), n)]

    def chip(dy, dz):
        return ((y + dy) % NY, (z + dz) % 2)

    def pieces(k):
        n = SOURCES[CHUNKS[k][1]] * PIECE[CHUNKS[k][0]]
        a, h = ENDS[k], n // 2
        return {H1: (0, h), H2: (h, h), A1: (0, a), A2: (n - a, a), MID: (a, n - 2 * a), ALL: (0, n)}

    plan = {
        0: (chip(0, 0), H1, up),
        1: (chip(0, 0), H2, up),
        2: (chip(0, 0), H2, down),
        3: (chip(0, 0), H1, down),
        4: (chip(0, 0), A1, side),
        5: (chip(0, 0), A2, side),
        6: (chip(0, 0), MID, side),
        7: (chip(3, 0), H1, up),
        8: (chip(1, 0), H2, down),
        9: (chip(0, 1), A1, up),
        10: (chip(0, 1), A2, up),
        11: (chip(0, 1), A2, down),
        12: (chip(0, 1), A1, down),
        13: (chip(3, 1), A1, up),
        14: (chip(1, 1), A2, down),
        15: (chip(3, 0), MID, side),
        16: (chip(1, 0), MID, side),
        17: (chip(2, 0), MID, side),
        18: (chip(0, 0), ALL, twin),
        19: (chip(0, 1), ALL, twin),
        20: (chip(3, 0), ALL, twin),
        21: (chip(1, 0), ALL, twin),
        22: (chip(2, 0), ALL, twin),
        23: (chip(3, 1), A1, twin),
        24: (chip(3, 1), A2, twin),
        25: (chip(1, 1), A2, twin),
        26: (chip(1, 1), A1, twin),
        27: (chip(2, 1), A1, twin),
        28: (chip(2, 1), A2, twin),
        29: (chip(3, 1), MID, twin),
        30: (chip(1, 1), MID, twin),
        31: (chip(2, 1), MID, twin),
    }
    came = {
        0: chip(3, 0), 1: chip(3, 0), 2: chip(1, 0), 3: chip(1, 0),
        4: chip(0, 1), 5: chip(0, 1), 6: chip(0, 1),
        7: chip(2, 0), 8: chip(2, 0),
        9: chip(3, 1), 10: chip(3, 1), 11: chip(1, 1), 12: chip(1, 1),
        13: chip(2, 1), 14: chip(2, 1),
        15: chip(3, 1), 16: chip(1, 1), 17: chip(2, 1),
    }

    def copy(k, tag, origin, core):
        _, piece, target = plan[tag]
        if k in WHOLE and tag > 22:
            piece = ALL
        ref = part(k, origin, core, *pieces(k)[piece])
        return pltpu.make_async_remote_copy(
            src_ref=ref,
            dst_ref=ref,
            send_sem=ssem.at[k, tag],
            recv_sem=rsem.at[k, tag],
            device_id=target,
            device_id_type=MESH,
        )

    def send(k, *tags):
        for t in tags:
            copy(k, t, plan[t][0], c).start()

    def wait(k, *tags):
        for t in tags:
            copy(k, t, came[t] if t < 18 else plan[t][0], c if t < 18 else 1 - c).wait_recv()

    def own(k):
        b, kind = CHUNKS[k]
        lot = 3 if kind == SAME else SOURCES[kind]
        if kind == SAME:
            pltpu.make_async_copy(stage[b].at[g], raw[b].at[y, c, zh, here[b]], own_sem.at[b]).wait()
        got = part(k, chip(0, 0), c, 0, lot * PIECE[b])
        pltpu.make_async_copy(got, got, in_sem.at[b, k % 3]).wait()
        send(k, 0, 2, 4, 5, 1, 3, 6, 18)

    def scale(b, dy, zs):
        if zs == 0:
            for k in range(3 * b, 3 * b + 3):
                wait(k, *(WHOLE_FROM_TWIN if k in WHOLE else FROM_TWIN)[dy])
        first, count = BATCHES[b]
        n, ys = PIECE[b], (y + dy) % NY

        def fetch(i, carry):
            cc, xs = i // NX, i % NX
            at_row = pl.ds(pl.multiple_of((zs * 4 + xs) * n, 16), n)
            to = rows.at[:, pl.ds(pl.multiple_of(i * 4 * ROWS, 16), 4 * ROWS), :]
            for gz in range(NZ):
                v = raw[b][ys, cc, gz, at_row, :].astype(jnp.float32)
                for e in range(count):
                    to[e, pl.ds(gz * ROWS, ROWS), :] = v[e * ROWS : (e + 1) * ROWS]
            return carry

        lax.fori_loop(0, CORES * NX, fetch, 0)
        row = lax.broadcasted_iota(jnp.int32, (16, QB), 0)

        def expert(e, carry):
            found = jnp.zeros((16, QB), jnp.float32)
            for blk in range(BLOCKS):
                v = rows[e, pl.ds(blk * QB, QB), :]
                m = jnp.max(jnp.max(jnp.abs(v), axis=0, keepdims=True), axis=1, keepdims=True) + 1e-06
                s = jnp.broadcast_to(m, (16, QB)).astype(jnp.bfloat16).astype(jnp.float32)
                buf[first + e, ys * 2 + zs, pl.ds(blk * QB, QB), :] = (v / s[0:1]).astype(jnp.bfloat16)
                found = jnp.where(row == blk, s, found)
            buf[first + e, ys * 2 + zs, pl.ds(SHARE, 16), :] = found.astype(jnp.bfloat16)
            return carry

        lax.fori_loop(0, count, expert, 0)

    def further(i):
        pl.semaphore_wait(ready.at[i], len(line) + 2 if i == 0 else 2)
        if i < 2:
            signal(ready.at[i + 1], [side, out])
        if i == 0:
            give(0, NEAR, zh + 3 + 2 * z, 1 - z, (2, 1, 3, 0))
        elif i == 1:
            give(0, NEAR, zh + 1 + 2 * z, z, (2, 1, 3, 0))
        else:
            give(0, AWAY, zh + 2, 1 - z, (2, 1, 3, 0))
            give(1, NEAR, zh + 3 + 2 * z, 1 - z, (2, 1, 3, 0))
            give(1, NEAR, zh + 1 + 2 * z, z, (2, 1, 3, 0))
            give(1, AWAY, zh + 2, 1 - z, (2, 1, 3, 0))

    pl.semaphore_wait(barrier, len(near))
    signal(ready.at[0], line + [side, out])
    for b in range(2):
        give(b, SAME, zh, z, (2, 1, 3))

    for step, k in ORDER:
        if step == ROUND:
            further(k)
        elif step == OWN:
            own(k)
        elif step == SCALE:
            scale(k // 8, k // 2 % NY, k % 2)
        else:
            first, then = (WHOLE_STEPS if k in WHOLE else STEPS)[step]
            wait(k, *first)
            send(k, *then)

    for k, (b, kind) in enumerate(CHUNKS):
        for t in range(TAGS):
            if k not in WHOLE or t < 23 or t in (23, 25, 27):
                copy(k, t, plan[t][0], c).wait_send()
        lot = 3 if kind == SAME else SOURCES[kind]
        gone = part(k, chip(0, 0), c, 0, lot * PIECE[b])
        pltpu.make_async_copy(gone, gone, out_sem.at[b, k % 3]).wait()


def place(slot_ref, buf, out_ref, scale_ref, found, sem, scale_sem):
    for s in range(EXPERTS):
        e = slot_ref[s]
        pltpu.make_async_copy(buf.at[e, :, pl.ds(0, SHARE)], out_ref.at[s], sem.at[s]).start()
    row = lax.broadcasted_iota(jnp.int32, (16, QB), 0)
    lane = lax.broadcasted_iota(jnp.int32, (16, QB), 1)
    lines = jnp.zeros((16, QB), jnp.float32)
    for s in range(EXPERTS):
        e = slot_ref[s]
        line = jnp.zeros((16, QB), jnp.float32)
        for ch in range(CHIPS):
            here = (lane - row == ch * BLOCKS) & (row < BLOCKS)
            line += jnp.where(here, buf[e, ch, pl.ds(SHARE, 16), :].astype(jnp.float32), 0.0)
        line = jnp.sum(line, axis=0, keepdims=True)
        lines = jnp.where(row == s, jnp.broadcast_to(line, (16, QB)), lines)
    found[...] = lines[:EXPERTS, : CHIPS * BLOCKS].astype(jnp.bfloat16)
    out = pltpu.make_async_copy(found, scale_ref, scale_sem)
    out.start()
    for s in range(EXPERTS):
        pltpu.make_async_copy(buf.at[0, :, pl.ds(0, SHARE)], out_ref.at[s], sem.at[s]).wait()
    out.wait()


def shards(trainer_gate, expert_of_slot):
    rest = [pltpu.VMEM((NY, CORES, NZ, 8 * n, QB), jnp.bfloat16) for n in PIECE]
    ready_to_go = [pltpu.VMEM((NX * NZ, n, QB), jnp.bfloat16) for n in PIECE]
    gathered = pl.pallas_call(
        spread,
        out_shape=pltpu.VMEM((EXPERTS, CHIPS, SHARE + 16, QB), jnp.bfloat16),
        in_specs=[pl.BlockSpec(memory_space=pl.ANY)],
        out_specs=pl.BlockSpec(memory_space=pltpu.VMEM),
        scratch_shapes=[
            pltpu.VMEM((EXPERTS, ROWS, FF), jnp.bfloat16),
            *ready_to_go,
            *rest,
            pltpu.VMEM((4, SHARE, QB), jnp.float32),
            pltpu.SemaphoreType.DMA,
            pltpu.SemaphoreType.DMA((2,)),
            pltpu.SemaphoreType.DMA((2, 3)),
            pltpu.SemaphoreType.DMA((2, 3)),
            pltpu.SemaphoreType.REGULAR((3,)),
            pltpu.SemaphoreType.DMA((len(CHUNKS), TAGS)),
            pltpu.SemaphoreType.DMA((len(CHUNKS), TAGS)),
        ],
        compiler_params=pltpu.CompilerParams(collective_id=0, has_side_effects=True, vmem_limit_bytes=52 * 2**20),
        name="spread",
    )(trainer_gate)
    placed, scales = pl.pallas_call(
        place,
        out_shape=(
            jax.ShapeDtypeStruct((EXPERTS, CHIPS, SHARE, QB), jnp.bfloat16),
            jax.ShapeDtypeStruct((EXPERTS, CHIPS * BLOCKS), jnp.bfloat16),
        ),
        in_specs=[
            pl.BlockSpec(memory_space=pltpu.SMEM),
            pl.BlockSpec(memory_space=pltpu.VMEM),
        ],
        out_specs=(pl.BlockSpec(memory_space=pl.ANY), pl.BlockSpec(memory_space=pl.ANY)),
        scratch_shapes=[
            pltpu.VMEM((EXPERTS, CHIPS * BLOCKS), jnp.bfloat16),
            pltpu.SemaphoreType.DMA((EXPERTS,)),
            pltpu.SemaphoreType.DMA,
        ],
        compiler_params=pltpu.CompilerParams(vmem_limit_bytes=20 * 2**20),
        name="place",
    )(expert_of_slot, gathered)
    return placed.reshape(EXPERTS, CHIPS * SHARE, QB), scales.reshape(EXPERTS, CHIPS * BLOCKS, 1)


def solution(mesh):
    return jax.shard_map(
        shards,
        mesh=mesh,
        in_specs=(P(None, ("rep", "grp"), None), P()),
        out_specs=(P(None, None, "grp"), P(None, None, "grp")),
        check_vma=False,
    )
```
